128 devices in a mesh: facade: 8 (over z, core), sensor: 16 (over x, y).
Axes of the slice: x: 4, y: 4, z: 4, core: 2. Of those that a mesh axis runs over, the one named last changes fastest.
Arguments:
- sky: bfloat16 [2305, 512], P(None, 'sensor'), may hold values from 0.19921875 to 5
- daylight: bfloat16 [512, 145, 2305], P(('facade', 'sensor')), may hold values from -0.125 to 0.125
- bsdf: bfloat16 [512, 145, 145], P(('facade', 'sensor')), may hold values from -0.5 to 0.5
- view: bfloat16 [128, 288, 145, 256], P('sensor', 'facade'), may hold values from -0.0390625 to 0.0390625
- visible: int32 [128, 288], P('sensor', 'facade'), may hold values from 0 to 63, as said below
- counts: int32 [128, 8], P('sensor', 'facade'), may hold values from 9 to 36, as said below
Outputs:
- illuminance: float32 [128, 256, 512], P(('sensor', 'facade'))
The draws below stay inside these ranges and needn't reach their ends.
Inputs may be any that keep to these rules, and one draw needn't show every extreme that they name: `visible`: ids are counted within a facade row; the group with id r belongs to the sensor index r // 4 of that row. Over the used slots of one sensor index's 8 blocks in one facade row, exactly 2 distinct groups of every source sensor index appear. Unused slots also name groups of the row. `counts`: in every facade row, some block of each sensor index uses all 36 slots.
All inputs are finite; a program needn't handle non-finite values.
Results may differ from the reference program's by a relative error of at most 0.0041.
Values may be sent and summed in bfloat16 or wider, within the bound.
A program may use at most 192 MiB of HBM per device.

```python
import math
import jax
import jax.numpy as jnp
from jax import lax

KLEMS = 145
PATCHES = 2305
SENS = 256
SLOTS = 36
CAP = 2
G_DEV = 4
SB_DEV = 8
HOURS = 512
ROW_GROUPS = 64
GROUPS = 512
SBLOCKS = 128
N_FACADE = 8
N_SENSOR = 16


def visibility_tables(key):
    key_count, key_top, key_cand, key_pick, key_cover = jax.random.split(key, 5)
    block_counts = jax.random.randint(key_count, (N_SENSOR, SB_DEV, N_FACADE), SLOTS // 4, SLOTS + 1)
    top_block = jax.random.randint(key_top, (N_SENSOR, N_FACADE), 0, SB_DEV)
    full = jnp.arange(SB_DEV)[None, :, None] == top_block[:, None, :]
    block_counts = jnp.where(full, SLOTS, block_counts).astype(jnp.int32)
    scores = jax.random.randint(key_cand, (N_SENSOR, N_FACADE, N_SENSOR, G_DEV), 0, 1 << 20)
    scores = scores * G_DEV + jnp.arange(G_DEV)[None, None, None, :]
    chosen_local = jnp.argsort(scores, axis=-1, stable=True)[..., :CAP]
    source_base = jnp.arange(N_SENSOR)[None, None, :, None] * G_DEV
    candidates = (source_base + chosen_local).reshape(N_SENSOR, N_FACADE, N_SENSOR * CAP)
    total_cands = N_SENSOR * CAP
    picks = jax.random.randint(key_pick, (N_SENSOR, N_FACADE, SB_DEV * SLOTS), 0, total_cands)
    limits = jnp.transpose(block_counts, (0, 2, 1))[..., None]
    valid = (jnp.arange(SLOTS)[None, None, None, :] < limits).reshape(N_SENSOR, N_FACADE, SB_DEV * SLOTS)
    ranks = jnp.cumsum(valid.astype(jnp.int32), axis=-1) - 1
    cover_scores = jax.random.randint(key_cover, (N_SENSOR, N_FACADE, total_cands), 0, 1 << 20)
    cover_scores = cover_scores * total_cands + jnp.arange(total_cands)[None, None, :]
    cover_order = jnp.argsort(cover_scores, axis=-1, stable=True)
    cover = jnp.take_along_axis(cover_order, jnp.clip(ranks, 0, total_cands - 1), axis=-1)
    picks = jnp.where(valid & (ranks < total_cands), cover, picks)
    ids = jnp.take_along_axis(candidates, picks, axis=-1)
    ids = ids.reshape(N_SENSOR, N_FACADE, SB_DEV, SLOTS)
    ids = jnp.transpose(ids, (0, 2, 1, 3)).reshape(N_SENSOR * SB_DEV, N_FACADE * SLOTS)
    return (ids.astype(jnp.int32), block_counts.reshape(N_SENSOR * SB_DEV, N_FACADE))


def draw_visible(key, part):
    tables = visibility_tables(key)
    return tables[0]


def draw_counts(key, part):
    tables = visibility_tables(key)
    return tables[1]


def raised(values, own_key, source, target, shards_of, factor):
    owner, partner = [(jnp.arange(values.shape[position]) // (values.shape[position] // shards_of)).reshape([-1 if axis == position else 1 for axis in range(values.ndim)]) for position in (source, target)]
    chosen = jax.random.permutation(own_key, shards_of)[partner]
    strong = (owner == chosen) | (owner == (partner + shards_of // 2) % shards_of)
    return jnp.where(strong, factor * values, values)


def block_scale(rng, shape, cuts, low, top_value):
    def one(position, blocks):
        steps = jax.random.uniform(jax.random.fold_in(jax.random.fold_in(rng, 6), position), (blocks,), jnp.float32, low / len(cuts), top_value / len(cuts))
        return jnp.repeat(jnp.exp(steps), shape[position] // blocks).reshape((-1,) + (1,) * (len(shape) - position - 1))

    loudness = one(*cuts[0])
    for cut in cuts[1:]:
        loudness = loudness * one(*cut)
    return loudness


def scatter_about(rng, dims, spread, reach, cuts=(), kind=jnp.bfloat16):
    loudness = block_scale(rng, dims, cuts, -0.22, 0.18) if cuts else 1.0
    array = jax.random.normal(rng, dims, jnp.float32) * spread * loudness
    return jnp.minimum(jnp.maximum(array, -reach), reach).astype(kind)


def bell_draw_with(rng, shape, width, bound, cuts, heavy, kind=jnp.bfloat16):
    entries = width * jax.random.normal(rng, shape, jnp.float32)
    if cuts:
        entries = entries * block_scale(rng, shape, cuts, -0.22, 0.18)
    return jnp.clip(raised(entries, jax.random.fold_in(rng, 3), *heavy), -bound, bound).astype(kind)


def setup_inputs(seed: int = 0) -> dict:
    key_of = jax.random.split(jax.random.key(seed), 7)
    return {
        "sky": jnp.clip(jnp.exp(math.log(5.0) - 3.2227897 * jax.random.uniform(key_of[0], (PATCHES, HOURS), jnp.float32) ** block_scale(key_of[0], (PATCHES, HOURS), ((1, 16),), -0.2, 0.2)), 0.19921875, 5.0).astype(jnp.bfloat16),
        "daylight": scatter_about(key_of[1], (GROUPS, KLEMS, PATCHES), PATCHES ** -0.5, 0.125, ((0, 128),)),
        "bsdf": scatter_about(key_of[2], (GROUPS, KLEMS, KLEMS), KLEMS ** -0.5, 0.5, ((0, 128),)),
        "view": bell_draw_with(key_of[3], (SBLOCKS, N_FACADE * SLOTS, KLEMS, SENS), (KLEMS * SLOTS * N_FACADE) ** -0.5, 0.0390625, ((0, 16), (1, 8)), (1, 0, 16, 2.0)),
        "visible": draw_visible(jax.random.fold_in(key_of[6], 71), 0),
        "counts": draw_counts(jax.random.fold_in(key_of[6], 71), 0),
    }


def reference(sky, daylight, bsdf, view, visible, counts):
    flat = daylight.reshape(GROUPS * KLEMS, PATCHES)
    daylit = jnp.dot(flat, sky, preferred_element_type=jnp.float32).astype(jnp.bfloat16)
    daylit = daylit.reshape(GROUPS, KLEMS, HOURS)
    exitance = jnp.einsum("gkl,glh->gkh", bsdf.astype(jnp.float32), daylit.astype(jnp.float32))
    exitance = exitance.astype(jnp.bfloat16)
    slot_index = jnp.arange(N_FACADE * SLOTS, dtype=jnp.int32)
    row_start = (slot_index // SLOTS) * ROW_GROUPS
    within = slot_index % SLOTS

    def one_block(item):
        block_view, block_ids, block_counts = item
        limits = jnp.repeat(block_counts, SLOTS)
        used = within < limits
        chosen = exitance[(row_start + block_ids).astype(jnp.int32)].astype(jnp.float32)
        chosen = jnp.where(used[:, None, None], chosen, jnp.zeros((), jnp.float32))
        return jnp.einsum("jks,jkh->sh", block_view.astype(jnp.float32), chosen)

    return lax.map(one_block, (view, visible, counts))
```

```python
import functools

import jax
import jax.numpy as jnp
from jax import lax
from jax.experimental import pallas as pl
from jax.experimental.pallas import tpu as pltpu
from jax.sharding import PartitionSpec as P

MESH = pl.DeviceIdType.MESH
BF = jnp.bfloat16
F32 = jnp.float32
I32 = jnp.int32

CHUNKS = 4
HC = 128
BUFS = 4


def iota(shape, dim):
    return lax.broadcasted_iota(I32, shape, dim)


def nt(a, b):
    return lax.dot_general(a, b, (((1,), (1,)), ((), ())), preferred_element_type=F32)


def mm(a, b):
    return jnp.dot(a, b, preferred_element_type=F32)


def kernel(sky, day, bsdf, view, vis_v, vis_s, cnt, out,
           skyv, dayv, bsdfv, bexp, vbuf, v2,
           e0, e1, e2, e3, m0, m1, m2, m3,
           s2m, s2r, r2r, trem, selb, selp, qsel, eidx, sels, rss, rsr, own, perm,
           lsem, vsem, k1s, k1r, k2s, k2r, kcs, kcr, ls_s, ls_r,
           p1s, p1r, p2ms, p2mr, p2rs, p2rr, rs_s, rs_r):
    e1buf = [e0, e1, e2, e3]
    r2m = [m0, m1, m2, m3]
    f = lax.axis_index("facade")
    s = lax.axis_index("sensor")
    z, o = f // 2, f % 2
    x, y = s // 4, s % 4
    a = x * (1 - o) + y * o
    b = y * (1 - o) + x * o

    def sid(i, j):
        i, j = i % 4, j % 4
        return (i * 4 + j) * (1 - o) + (j * 4 + i) * o

    def first(d):
        return (f, sid(a + d, b))

    def second(d):
        return (f, sid(a, b + d))

    partner = (z * 2 + (1 - o), s)
    sends = []

    def push(src, dst, ss, rs, dev):
        cp = pltpu.make_async_remote_copy(src_ref=src, dst_ref=dst, send_sem=ss, recv_sem=rs,
                                          device_id=dev, device_id_type=MESH)
        cp.start()
        sends.append(cp)

    def arrived(dst, ss, rs, dev):
        pltpu.make_async_remote_copy(src_ref=dst, dst_ref=dst, send_sem=ss, recv_sem=rs,
                                     device_id=dev, device_id_type=MESH).wait_recv()

    c_sky = pltpu.make_async_copy(sky, skyv.at[s], lsem.at[0])
    c_sky.start()
    c_day = pltpu.make_async_copy(day, dayv, lsem.at[1])
    c_day.start()
    c_bs = pltpu.make_async_copy(bsdf, bsdfv, lsem.at[2])
    c_bs.start()

    def view_copy(j, slot):
        return pltpu.make_async_copy(view.at[j], vbuf.at[slot, pl.ds(0, 145)], vsem.at[slot])

    for q in range(BUFS):
        vbuf[q, 145:160] = jnp.zeros((15, 8, 256), BF)
        view_copy(q, q).start()

    barrier = pltpu.get_barrier_semaphore()
    for d in (1, 2, 3):
        pl.semaphore_signal(barrier, inc=1, device_id=first(d), device_id_type=MESH)
        pl.semaphore_signal(barrier, inc=1, device_id=second(d), device_id_type=MESH)
    for d in range(1, 8):
        pl.semaphore_signal(barrier, inc=1, device_id=((f + d) % 8, s), device_id_type=MESH)
    pl.semaphore_wait(barrier, 13)

    half = pl.ds(pl.multiple_of(16 * o, 16), 16)
    other = pl.ds(pl.multiple_of(16 * (1 - o), 16), 16)
    c_sky.wait()
    for d in (1, 3, 2):
        r = skyv.at[s, half]
        push(r, r, k1s.at[d], k1r.at[d], first(d))
    for d in (1, 2, 3):
        r = skyv.at[s, half]
        push(r, r, k2s.at[d, 0], k2r.at[d, 0], second(d))

    vis = vis_v[...]
    slot_no = iota((8, 36), 1)
    row_no = iota((8, 36), 0)
    lim = jnp.zeros((8, 36), I32)
    for q in range(8):
        lim = jnp.where(row_no == q, cnt[0, q], lim)
    used = slot_no < lim
    src = vis >> 2
    grp = vis & 3
    for q in range(16):
        hit = used & (src == q)
        lo = jnp.min(jnp.where(hit, grp, 3))
        hi = jnp.max(jnp.where(hit, grp, 0))
        sels[2 * q] = lo
        sels[2 * q + 1] = hi
        selb[2 * q:2 * q + 1, :] = jnp.full((1, 128), lo, I32)
        selb[2 * q + 1:2 * q + 2, :] = jnp.full((1, 128), hi, I32)
    for d in (1, 2, 3):
        push(selb, selp.at[4 - d], ls_s.at[d], ls_r.at[4 - d], second(d))

    c_bs.wait()
    w1 = (iota((580, 145), 0) // 4 == iota((580, 145), 1)).astype(F32).astype(BF)
    c1 = nt(w1, bsdfv[...]).astype(BF)
    pr, pc = iota((580, 640), 0), iota((580, 640), 1)
    pk, pg = pr // 4, pr % 4
    hit = (pc < 512) & (pc == pg * 128 + pk) & (pk < 128)
    hit = hit | ((pk >= 128) & (pc - 512 == 17 * pg + pk - 128))
    c2 = mm(c1, hit.astype(F32).astype(BF))
    rr = pc - 512
    gcol = jnp.where(pc < 512, pc // 128,
                     (rr >= 17).astype(I32) + (rr >= 34).astype(I32) + (rr >= 51).astype(I32))
    bexp[...] = jnp.where(pg == gcol, c2, 0.0).astype(BF)

    ur, uc = iota((256, 256), 0), iota((256, 256), 1)
    perm[...] = ((uc % 8 == ur // 32) & (uc // 8 == ur % 32)).astype(F32).astype(BF)

    for d in (1, 3, 2):
        n = sid(a - d, b)
        r = skyv.at[n, half]
        arrived(r, k1s.at[d], k1r.at[d], first(d))
        for dd in (1, 2, 3):
            push(r, r, k2s.at[dd, d], k2r.at[dd, d], second(dd))
        push(r, r, kcs.at[0, d], kcr.at[0, d], partner)
    c_day.wait()

    def permute(lo, hi):
        def body(j, carry):
            slot = j % BUFS
            view_copy(j, slot).wait()
            for t in range(5):
                xin = vbuf[slot, 32 * t:32 * t + 32].reshape(256, 256)
                res = mm(perm[...], xin).astype(BF)
                v2[j, :, 32 * t:32 * t + 32, :] = res.reshape(8, 32, 256)

            @pl.when(j + BUFS < 36)
            def _():
                view_copy(j + BUFS, slot).start()
            return carry
        lax.fori_loop(lo, hi, body, 0)

    permute(0, 8)

    for d in (1, 3, 2):
        for i in range(4):
            r = skyv.at[sid(a - i, b - d), half]
            arrived(r, k2s.at[d, i], k2r.at[d, i], second(d))
            push(r, r, kcs.at[d, i], kcr.at[d, i], partner)
    for d in range(4):
        for i in range(4):
            if d or i:
                r = skyv.at[sid(a - d, b - i), other]
                arrived(r, kcs.at[d, i], kcr.at[d, i], partner)

    def daylit(c):
        lhs = skyv[4 * c:4 * c + 4].reshape(HC, 2305)
        dt = nt(lhs, dayv[...]).astype(BF)
        e = mm(dt, bexp[...]).astype(BF)
        for q in range(5):
            e1buf[c][a, q] = e[:, 128 * q:128 * q + 128]
        r = e1buf[c].at[a]
        for d in (1, 3, 2):
            push(r, r, p1s.at[c, d], p1r.at[c, d], first(d))

    def make_q(d):
        lane, col = iota((128, 256), 0), iota((128, 256), 1)
        for i in range(4):
            acc = jnp.zeros((128, 256), F32)
            for m in range(2):
                row = sid(i, b) * 2 + m
                sel = selp[d, pl.ds(row, 1), :]
                sel = jnp.concatenate([sel, sel], axis=1)
                n = 2 * i + m
                c0 = 17 * n if n < 7 else 128
                hit = (lane - col == 17 * sel - c0) & (col >= c0) & (col < c0 + 17)
                acc = acc + hit.astype(F32)
            qsel[d, 128 * i:128 * i + 128, :] = acc.astype(BF)

    def select(c):
        for d in (1, 3, 2):
            arrived(e1buf[c].at[(a - d) % 4], p1s.at[c, d], p1r.at[c, d], first(d))
        lhs = jnp.concatenate([e1buf[c][i, 4] for i in range(4)], axis=1)
        for d in (2, 1, 3, 0):
            rem = mm(lhs, qsel[d]).astype(BF)
            for i in range(4):
                planes = [e1buf[c][i, g] for g in range(4)]
                for m in range(2):
                    row = sid(i, b) * 2 + m
                    sel = selp[d, pl.ds(row, 1), :]
                    pick = planes[0]
                    for g in range(1, 4):
                        pick = jnp.where(sel == g, planes[g].astype(F32), pick.astype(F32)).astype(BF)
                    if d:
                        s2m[c, d, 2 * i + m] = pick
                    else:
                        r2m[c][b * 8 + 2 * i + m] = pick
            if d:
                s2r[c, d, 0] = rem[:, :128]
                s2r[c, d, 1] = rem[:, 128:]
                push(s2m.at[c, d], r2m[c].at[pl.ds(b * 8, 8)], p2ms.at[c, d], p2mr.at[c, d], second(d))
                push(s2r.at[c, d], r2r.at[c, b], p2rs.at[c, d], p2rr.at[c, d], second(d))
            else:
                r2r[c, b, 0] = rem[:, :128]
                r2r[c, b, 1] = rem[:, 128:]

    def received(c):
        for d in (1, 3, 2):
            j = (b - d) % 4
            arrived(r2m[c].at[pl.ds(j * 8, 8)], p2ms.at[c, d], p2mr.at[c, d], second(d))
            arrived(r2r.at[c, j], p2rs.at[c, d], p2rr.at[c, d], second(d))
        keep = iota((HC, 128), 1) < 17

        def body(fb, carry):
            plane = r2r[c, fb, 0].astype(F32)
            for n in range(7):
                v = plane if n == 0 else pltpu.roll(plane, 128 - 17 * n, 1)
                trem[fb * 8 + n] = jnp.where(keep, v, 0.0).astype(BF)
            trem[fb * 8 + 7] = r2r[c, fb, 1]
            return carry
        lax.fori_loop(0, 4, body, 0)

    def compute(c):
        def block(i):
            bb = (f + 1 + i) % 8
            acc = None
            for j in range(36):
                e = eidx[bb * 36 + j]
                lhs = jnp.concatenate([r2m[c][e], trem[e]], axis=1)[:, :160]
                p = mm(lhs, v2[j, bb])
                acc = p if acc is None else acc + p
            return acc

        def body(i, carry):
            rss[c, i] = block(i).astype(BF)
            rs_copy(c, i).start()
            return carry
        lax.fori_loop(0, 7, body, 0)
        own[c] = block(7)

    def rs_copy(c, i):
        return pltpu.make_async_remote_copy(
            src_ref=rss.at[c, i], dst_ref=rsr.at[c, i], send_sem=rs_s.at[c, i], recv_sem=rs_r.at[c, i],
            device_id=((f + 1 + i) % 8, s), device_id_type=MESH)

    def reduce(c):
        def body(i, carry):
            rs_copy(c, i).wait_recv()
            own[c] += rsr[c, i].astype(F32)
            return carry
        lax.fori_loop(0, 7, body, 0)
        out[0, :, HC * c:HC * c + HC] = own[c].T

    daylit(0)
    daylit(1)
    for c in range(CHUNKS):
        r2m[c][32] = jnp.zeros((HC, 128), BF)
    trem[32] = jnp.zeros((HC, 128), BF)

    def entries(n, carry):
        bb, j = n // 36, n % 36
        v = vis_s[bb, j]
        sx, sy, g = v // 16, (v // 4) % 4, v % 4
        m = jnp.where(g == sels[2 * (v // 4) + 1], 1, 0)
        ia = sx * (1 - o) + sy * o
        fb = sy * (1 - o) + sx * o
        eidx[n] = jnp.where(j < cnt[0, bb], fb * 8 + ia * 2 + m, 32)
        return carry
    lax.fori_loop(0, 288, entries, 0)

    selp[0] = selb[...]
    for d in (1, 2, 3):
        arrived(selp.at[d], ls_s.at[d], ls_r.at[d], second(d))
    for d in range(4):
        make_q(d)
    select(0)
    daylit(2)
    permute(8, 16)
    select(1)
    daylit(3)
    permute(16, 26)
    select(2)
    permute(26, 36)
    select(3)
    for c in range(CHUNKS):
        received(c)
        compute(c)
        if c:
            reduce(c - 1)
    reduce(CHUNKS - 1)
    for cp in sends:
        cp.wait_send()

    def drain(n, carry):
        rs_copy(n // 7, n % 7).wait_send()
        return carry
    lax.fori_loop(0, 7 * CHUNKS, drain, 0)


def on_device(sky, daylight, bsdf, view, visible, counts):
    skyt = sky.T
    day = daylight.transpose(1, 0, 2).reshape(580, 2305)
    bs = bsdf.transpose(1, 0, 2).reshape(580, 145)
    vw = view.transpose(1, 2, 0, 3)
    cnt = counts.T
    V = pltpu.VMEM
    D = pltpu.SemaphoreType.DMA
    anyspec = pl.BlockSpec(memory_space=pl.ANY)
    vm = pl.BlockSpec(memory_space=pltpu.VMEM)
    sm = pl.BlockSpec(memory_space=pltpu.SMEM)
    return pl.pallas_call(
        kernel,
        out_shape=jax.ShapeDtypeStruct((1, 256, 512), F32),
        in_specs=[anyspec, anyspec, anyspec, anyspec, vm, sm, sm],
        out_specs=vm,
        scratch_shapes=[
            V((16, 32, 2305), BF), V((580, 2305), BF), V((580, 145), BF), V((580, 640), BF),
            V((BUFS, 160, 8, 256), BF), V((36, 8, 160, 256), BF),
            *[V((4, 5, HC, 128), BF)] * 4, *[V((33, HC, 128), BF)] * 4,
            V((CHUNKS, 4, 8, HC, 128), BF), V((CHUNKS, 4, 2, HC, 128), BF),
            V((CHUNKS, 4, 2, HC, 128), BF), V((33, HC, 128), BF),
            V((32, 128), I32), V((4, 32, 128), I32), V((4, 512, 256), BF),
            pltpu.SMEM((288,), I32), pltpu.SMEM((32,), I32),
            V((CHUNKS, 7, HC, 256), BF), V((CHUNKS, 7, HC, 256), BF), V((CHUNKS, HC, 256), F32),
            V((256, 256), BF),
            D((3,)), D((BUFS,)), D((4,)), D((4,)), D((4, 4)), D((4, 4)), D((4, 4)), D((4, 4)),
            D((4,)), D((4,)),
            *[D((CHUNKS, 4))] * 6, D((CHUNKS, 7)), D((CHUNKS, 7)),
        ],
        compiler_params=pltpu.CompilerParams(
            collective_id=0, has_side_effects=True, vmem_limit_bytes=60 * 2**20),
    )(skyt, day, bs, vw, visible, visible, cnt)


def solution(mesh):
    placed = (
        P(None, "sensor"),
        P(("facade", "sensor"), None, None),
        P(("facade", "sensor"), None, None),
        P("sensor", "facade", None, None),
        P("sensor", "facade"),
        P("sensor", "facade"),
    )
    return jax.shard_map(
        on_device,
        mesh=mesh,
        in_specs=placed,
        out_specs=P(("sensor", "facade"), None, None),
        check_vma=False,
    )
```

```python
import functools

import jax
import jax.numpy as jnp
from jax import lax
from jax.experimental import pallas as pl
from jax.experimental.pallas import tpu as pltpu
from jax.sharding import PartitionSpec as P

MESH = pl.DeviceIdType.MESH
BF = jnp.bfloat16
F32 = jnp.float32
I32 = jnp.int32

CHUNKS = 4
HC = 128
BUFS = 4


def iota(shape, dim):
    return lax.broadcasted_iota(I32, shape, dim)


def nt(a, b):
    return lax.dot_general(a, b, (((1,), (1,)), ((), ())), preferred_element_type=F32)


def mm(a, b):
    return jnp.dot(a, b, preferred_element_type=F32)


def kernel(sky, day, bsdf, view, vis_v, cnt, out,
           skyv, rawd, rawb, dayv, bsdfv, bexp, vbuf, v2,
           e0, e1, e2, e3, m0, m1, m2, m3,
           s2m, s2r, r2r, trem, selb, selp, qsel, qrest, ent, eidx, rss, rsr, own, perm,
           lsem, vsem, k1s, k1r, k2s, k2r, kcs, kcr, ls_s, ls_r,
           p1s, p1r, p2ms, p2mr, p2rs, p2rr, rs_s, rs_r):
    e1buf = [e0, e1, e2, e3]
    r2m = [m0, m1, m2, m3]
    f = lax.axis_index("facade")
    s = lax.axis_index("sensor")
    z, o = f // 2, f % 2
    x, y = s // 4, s % 4
    a = x * (1 - o) + y * o
    b = y * (1 - o) + x * o

    def sid(i, j):
        i, j = i % 4, j % 4
        return (i * 4 + j) * (1 - o) + (j * 4 + i) * o

    def first(d):
        return (f, sid(a + d, b))

    def second(d):
        return (f, sid(a, b + d))

    partner = (z * 2 + (1 - o), s)
    sends = []

    def push(src, dst, ss, rs, dev):
        cp = pltpu.make_async_remote_copy(src_ref=src, dst_ref=dst, send_sem=ss, recv_sem=rs,
                                          device_id=dev, device_id_type=MESH)
        cp.start()
        sends.append(cp)

    def arrived(dst, ss, rs, dev):
        pltpu.make_async_remote_copy(src_ref=dst, dst_ref=dst, send_sem=ss, recv_sem=rs,
                                     device_id=dev, device_id_type=MESH).wait_recv()

    def piece(i, j):
        i, j = i % 4, j % 4
        return skyv.at[o, (i + j) % 4, j * (1 - o) + i * o]

    c_sky = pltpu.make_async_copy(sky.at[pl.ds(pl.multiple_of(16 * o, 16), 16)], piece(a, b), lsem.at[0])
    c_sky.start()
    c_bs = pltpu.make_async_copy(bsdf, rawb, lsem.at[2])
    c_bs.start()
    c_day = pltpu.make_async_copy(day, rawd, lsem.at[1])
    c_day.start()

    def view_copy(j, slot):
        return pltpu.make_async_copy(view.at[j], vbuf.at[slot, pl.ds(0, 145)], vsem.at[slot])

    for q in range(BUFS):
        vbuf[q, 145:160] = jnp.zeros((15, 8, 256), BF)
        view_copy(q, q).start()

    barrier = pltpu.get_barrier_semaphore()
    for d in (1, 2, 3):
        pl.semaphore_signal(barrier, inc=1, device_id=first(d), device_id_type=MESH)
        pl.semaphore_signal(barrier, inc=1, device_id=second(d), device_id_type=MESH)
    for d in range(1, 8):
        pl.semaphore_signal(barrier, inc=1, device_id=((f + d) % 8, s), device_id_type=MESH)
    pl.semaphore_wait(barrier, 13)

    c_sky.wait()
    for d in (2, 1, 3):
        r = piece(a, b)
        push(r, r, k1s.at[d], k1r.at[d], first(d))

    vis = vis_v[...]
    slot_no = iota((8, 36), 1)
    row_no = iota((8, 36), 0)
    lim = jnp.zeros((8, 36), I32)
    for q in range(8):
        lim = jnp.where(row_no == q, cnt[0, q], lim)
    used = slot_no < lim
    src = vis >> 2
    grp = vis & 3
    later = jnp.zeros((8, 36), I32)
    for q in range(16):
        hit = used & (src == q)
        lo = jnp.min(jnp.where(hit, grp, 3))
        hi = jnp.max(jnp.where(hit, grp, 0))
        selb[2 * q:2 * q + 1, :] = jnp.full((1, 128), lo, I32)
        selb[2 * q + 1:2 * q + 2, :] = jnp.full((1, 128), hi, I32)
        later = jnp.where(hit & (grp == hi), 1, later)
    for d in (1, 2, 3):
        push(selb, selp.at[4 - d], ls_s.at[d], ls_r.at[4 - d], second(d))
    sx, sy = src >> 2, src & 3
    ia = sx * (1 - o) + sy * o
    fb = sy * (1 - o) + sx * o
    ent[...] = jnp.zeros((8, 128), I32)
    ent[:, 0:36] = jnp.where(used, fb * 8 + ia * 2 + later, 32)
    c_ent = pltpu.make_async_copy(ent, eidx, lsem.at[0])
    c_ent.start()

    c_day.wait()
    for t in range(9):
        dayv[64 * t:64 * t + 64, :] = rawd[16 * t:16 * t + 16].reshape(64, 2305)
    dayv[576:580, :] = rawd[144]

    for d in (1, 3, 2):
        arrived(piece(a - d, b), k1s.at[d], k1r.at[d], first(d))
    for c in range(CHUNKS):
        for d in (2, 1, 3):
            r = piece(c - b + 4, b)
            push(r, r, k2s.at[d, c], k2r.at[d, c], second(d))

    c_bs.wait()
    for t in range(9):
        bsdfv[64 * t:64 * t + 64, :] = rawb[16 * t:16 * t + 16].reshape(64, 145)
    bsdfv[576:580, :] = rawb[144]
    w1 = (iota((580, 145), 0) // 4 == iota((580, 145), 1)).astype(F32).astype(BF)
    c1 = nt(w1, bsdfv[...]).astype(BF)
    pr, pc = iota((580, 640), 0), iota((580, 640), 1)
    pk, pg = pr // 4, pr % 4
    hit = (pc < 512) & (pc == pg * 128 + pk) & (pk < 128)
    hit = hit | ((pk >= 128) & (pc - 512 == 17 * pg + pk - 128))
    c2 = mm(c1, hit.astype(F32).astype(BF))
    rr = pc - 512
    gcol = jnp.where(pc < 512, pc // 128,
                     (rr >= 17).astype(I32) + (rr >= 34).astype(I32) + (rr >= 51).astype(I32))
    bexp[...] = jnp.where(pg == gcol, c2, 0.0).astype(BF)

    ur, uc = iota((256, 256), 0), iota((256, 256), 1)
    perm[...] = ((uc % 8 == ur // 32) & (uc // 8 == ur % 32)).astype(F32).astype(BF)

    def permute(lo, hi):
        def body(j, carry):
            slot = j % BUFS
            view_copy(j, slot).wait()
            for t in range(5):
                xin = vbuf[slot, 32 * t:32 * t + 32].reshape(256, 256)
                res = mm(perm[...], xin).astype(BF)
                v2[j, :, 32 * t:32 * t + 32, :] = res.reshape(8, 32, 256)

            @pl.when(j + BUFS < 36)
            def _():
                view_copy(j + BUFS, slot).start()
            return carry
        lax.fori_loop(lo, hi, body, 0)

    def gather(c):
        for d in (1, 3, 2):
            arrived(piece(c - b + d + 4, b - d), k2s.at[d, c], k2r.at[d, c], second(d))
        r = skyv.at[o, c]
        push(r, r, kcs.at[c], kcr.at[c], partner)

    def daylit(c):
        arrived(skyv.at[1 - o, c], kcs.at[c], kcr.at[c], partner)
        lhs = jnp.concatenate([skyv[h, c, q] for q in range(4) for h in range(2)], axis=0)
        dt = nt(lhs, dayv[...]).astype(BF)
        e = mm(dt, bexp[...]).astype(BF)
        for q in range(5):
            e1buf[c][a, q] = e[:, 128 * q:128 * q + 128]
        r = e1buf[c].at[a]
        for d in (2, 1, 3):
            push(r, r, p1s.at[c, d], p1r.at[c, d], first(d))

    def make_q(d):
        lane, col = iota((128, 128), 0), iota((128, 128), 1)
        for i in range(4):
            acc = jnp.zeros((128, 128), F32)
            for m in range(2):
                n = 2 * i + m
                if n < 7:
                    sel = selp[d, pl.ds(sid(i, b) * 2 + m, 1), :]
                    hit = (lane - col == 17 * sel - 17 * n) & (col >= 17 * n) & (col < 17 * n + 17)
                    acc = acc + hit.astype(F32)
            qsel[d, 128 * i:128 * i + 128, :] = acc.astype(BF)
        row, lan = iota((32, 128), 0), iota((32, 128), 1)
        sel = selp[d, pl.ds(sid(3, b) * 2 + 1, 1), :]
        qrest[d] = ((lan - row == 17 * sel) & (row < 17)).astype(F32).astype(BF)

    def select(c):
        for d in (1, 3, 2):
            arrived(e1buf[c].at[(a - d) % 4], p1s.at[c, d], p1r.at[c, d], first(d))
        lhs = jnp.concatenate([e1buf[c][i, 4] for i in range(4)], axis=1)
        for d in (2, 1, 3, 0):
            for i in range(4):
                planes = [e1buf[c][i, g].astype(F32) for g in range(4)]
                for m in range(2):
                    sel = selp[d, pl.ds(sid(i, b) * 2 + m, 1), :]
                    pick = planes[0]
                    for g in range(1, 4):
                        pick = jnp.where(sel == g, planes[g], pick)
                    pick = pick.astype(BF)
                    if d:
                        s2m[c, d - 1, 2 * i + m] = pick
                    else:
                        r2m[c][b * 8 + 2 * i + m] = pick
            if d:
                push(s2m.at[c, d - 1], r2m[c].at[pl.ds(b * 8, 8)], p2ms.at[c, d], p2mr.at[c, d], second(d))
            rem = mm(lhs, qsel[d]).astype(BF)
            rest = nt(qrest[d], e1buf[c][3, 4]).astype(BF)
            if d:
                s2r[c, d - 1, 0:128] = rem
                s2r[c, d - 1, 128:160] = rest
                push(s2r.at[c, d - 1], r2r.at[c, b], p2rs.at[c, d], p2rr.at[c, d], second(d))
            else:
                r2r[c, b, 0:128] = rem
                r2r[c, b, 128:160] = rest

    def received(c):
        for d in (1, 3, 2):
            j = (b - d) % 4
            arrived(r2m[c].at[pl.ds(j * 8, 8)], p2ms.at[c, d], p2mr.at[c, d], second(d))
            arrived(r2r.at[c, j], p2rs.at[c, d], p2rr.at[c, d], second(d))
        keep = iota((HC, 128), 1) < 17
        eye = (iota((HC, HC), 0) == iota((HC, HC), 1)).astype(F32).astype(BF)

        def body(fb, carry):
            plane = r2r[c, fb, 0:128].astype(F32)
            for n in range(7):
                v = plane if n == 0 else pltpu.roll(plane, 128 - 17 * n, 1)
                trem[fb * 8 + n] = jnp.where(keep, v, 0.0)[:, :32].astype(BF)
            trem[fb * 8 + 7] = nt(eye, r2r[c, fb, 128:160]).astype(BF)
            return carry
        lax.fori_loop(0, 4, body, 0)

    def compute(c):
        def block(i):
            bb = (f + 1 + i) % 8
            acc = None
            for j in range(36):
                e = eidx[bb, j]
                lhs = jnp.concatenate([r2m[c][e], trem[e]], axis=1)
                p = mm(lhs, v2[j, bb])
                acc = p if acc is None else acc + p
            return acc

        def body(i, carry):
            rss[c, i] = block(i).astype(BF)
            pltpu.make_async_remote_copy(
                src_ref=rss.at[c, i], dst_ref=rsr.at[c, i], send_sem=rs_s.at[c], recv_sem=rs_r.at[c],
                device_id=((f + 1 + i) % 8, s), device_id_type=MESH).start()
            return carry
        lax.fori_loop(0, 7, body, 0)
        own[c] = block(7)

    def rs_all(c):
        return pltpu.make_async_remote_copy(
            src_ref=rss.at[c], dst_ref=rsr.at[c], send_sem=rs_s.at[c], recv_sem=rs_r.at[c],
            device_id=((f + 1) % 8, s), device_id_type=MESH)

    def reduce(c):
        rs_all(c).wait_recv()
        acc = own[c]
        for i in range(7):
            acc = acc + rsr[c, i].astype(F32)
        t = acc.T
        for q in range(4):
            lo = 128 * ((c - q) % 4) + 32 * q
            out[0, :, lo:lo + 32] = t[:, 32 * q:32 * q + 32]

    for c in range(CHUNKS):
        r2m[c][32] = jnp.zeros((HC, 128), BF)
    trem[32] = jnp.zeros((HC, 32), BF)
    permute(0, 10)
    gather(0)
    gather(1)
    daylit(0)
    gather(2)
    daylit(1)
    gather(3)
    selp[0] = selb[...]
    for d in (1, 2, 3):
        arrived(selp.at[d], ls_s.at[d], ls_r.at[d], second(d))
    for d in range(4):
        make_q(d)
    permute(10, 14)
    select(0)
    daylit(2)
    permute(14, 20)
    select(1)
    daylit(3)
    permute(20, 28)
    select(2)
    permute(28, 36)
    c_ent.wait()
    received(0)
    compute(0)
    select(3)
    for c in range(1, CHUNKS):
        received(c)
        compute(c)
        reduce(c - 1)
    reduce(CHUNKS - 1)
    for cp in sends:
        cp.wait_send()
    for c in range(CHUNKS):
        rs_all(c).wait_send()


def on_device(sky, daylight, bsdf, view, visible, counts):
    V = pltpu.VMEM
    D = pltpu.SemaphoreType.DMA
    anyspec = pl.BlockSpec(memory_space=pl.ANY)
    vm = pl.BlockSpec(memory_space=pltpu.VMEM)
    sm = pl.BlockSpec(memory_space=pltpu.SMEM)
    return pl.pallas_call(
        kernel,
        out_shape=jax.ShapeDtypeStruct((1, 256, 512), F32),
        in_specs=[anyspec, anyspec, anyspec, anyspec, vm, sm],
        out_specs=vm,
        scratch_shapes=[
            V((2, 4, 4, 16, 2305), BF), V((145, 4, 2305), BF), V((145, 4, 145), BF),
            V((580, 2305), BF), V((580, 145), BF), V((580, 640), BF),
            V((BUFS, 160, 8, 256), BF), V((36, 8, 160, 256), BF),
            *[V((4, 5, HC, 128), BF)] * 4, *[V((33, HC, 128), BF)] * 4,
            V((CHUNKS, 3, 8, HC, 128), BF), V((CHUNKS, 3, 160, 128), BF),
            V((CHUNKS, 4, 160, 128), BF), V((33, HC, 32), BF),
            V((32, 128), I32), V((4, 32, 128), I32), V((4, 512, 128), BF), V((4, 32, 128), BF),
            V((8, 128), I32), pltpu.SMEM((8, 128), I32),
            V((CHUNKS, 7, HC, 256), BF), V((CHUNKS, 7, HC, 256), BF), V((CHUNKS, HC, 256), F32),
            V((256, 256), BF),
            D((3,)), D((BUFS,)), D((4,)), D((4,)), D((4, 4)), D((4, 4)), D((4,)), D((4,)),
            D((4,)), D((4,)),
            *[D((CHUNKS, 4))] * 6, D((CHUNKS,)), D((CHUNKS,)),
        ],
        compiler_params=pltpu.CompilerParams(
            collective_id=0, has_side_effects=True, vmem_limit_bytes=60 * 2**20),
    )(sky.T, daylight.transpose(1, 0, 2), bsdf.transpose(1, 0, 2), view.transpose(1, 2, 0, 3),
      visible, counts.T)


def solution(mesh):
    placed = (
        P(None, "sensor"),
        P(("facade", "sensor"), None, None),
        P(("facade", "sensor"), None, None),
        P("sensor", "facade", None, None),
        P("sensor", "facade"),
        P("sensor", "facade"),
    )
    return jax.shard_map(
        on_device,
        mesh=mesh,
        in_specs=placed,
        out_specs=P(("sensor", "facade"), None, None),
        check_vma=False,
    )
```

```python
import functools

import jax
import jax.numpy as jnp
from jax import lax
from jax.experimental import pallas as pl
from jax.experimental.pallas import tpu as pltpu
from jax.sharding import PartitionSpec as P

MESH = pl.DeviceIdType.MESH
BF = jnp.bfloat16
F32 = jnp.float32
I32 = jnp.int32

CHUNKS = 4
HC = 128
BUFS = 4


def iota(shape, dim):
    return lax.broadcasted_iota(I32, shape, dim)


def nt(a, b):
    return lax.dot_general(a, b, (((1,), (1,)), ((), ())), preferred_element_type=F32)


def mm(a, b):
    return jnp.dot(a, b, preferred_element_type=F32)


def kernel(sky, day, bsdf, view, vis_v, cnt, out,
           skyv, rawd, rawb, dayv, bsdfv, bexp, vbuf, v2m, v2r,
           e0, e1, e2, e3, m0, m1, m2, m3,
           s2m, s2r, r2r, trem, selb, selp, qsel, qrest, place, ent, eidx, rss, rsr, own, perm,
           lsem, vsem, k1s, k1r, k2s, k2r, kcs, kcr, ls_s, ls_r,
           p1s, p1r, p2ms, p2mr, p2rs, p2rr, rs_s, rs_r):
    e1buf = [e0, e1, e2, e3]
    r2m = [m0, m1, m2, m3]
    f = lax.axis_index("facade")
    s = lax.axis_index("sensor")
    z, o = f // 2, f % 2
    x, y = s // 4, s % 4
    a = x * (1 - o) + y * o
    b = y * (1 - o) + x * o

    def sid(i, j):
        i, j = i % 4, j % 4
        return (i * 4 + j) * (1 - o) + (j * 4 + i) * o

    def first(d):
        return (f, sid(a + d, b))

    def second(d):
        return (f, sid(a, b + d))

    partner = (z * 2 + (1 - o), s)
    sends = []

    def push(src, dst, ss, rs, dev):
        cp = pltpu.make_async_remote_copy(src_ref=src, dst_ref=dst, send_sem=ss, recv_sem=rs,
                                          device_id=dev, device_id_type=MESH)
        cp.start()
        sends.append(cp)

    def arrived(dst, ss, rs, dev):
        pltpu.make_async_remote_copy(src_ref=dst, dst_ref=dst, send_sem=ss, recv_sem=rs,
                                     device_id=dev, device_id_type=MESH).wait_recv()

    def piece(i, j):
        i, j = i % 4, j % 4
        return skyv.at[o, (i + j) % 4, j * (1 - o) + i * o]

    c_sky = pltpu.make_async_copy(sky.at[pl.ds(pl.multiple_of(16 * o, 16), 16)], piece(a, b), lsem.at[0])
    c_sky.start()
    c_bs = pltpu.make_async_copy(bsdf, rawb, lsem.at[2])
    c_bs.start()
    c_day = pltpu.make_async_copy(day, rawd, lsem.at[1])
    c_day.start()

    def view_copy(j, slot):
        return pltpu.make_async_copy(view.at[j], vbuf.at[slot, pl.ds(0, 145)], vsem.at[slot])

    for q in range(BUFS):
        vbuf[q, 145:160] = jnp.zeros((15, 8, 256), BF)
        view_copy(q, q).start()

    barrier = pltpu.get_barrier_semaphore()
    for d in (1, 2, 3):
        pl.semaphore_signal(barrier, inc=1, device_id=first(d), device_id_type=MESH)
        pl.semaphore_signal(barrier, inc=1, device_id=second(d), device_id_type=MESH)
    for d in range(1, 8):
        pl.semaphore_signal(barrier, inc=1, device_id=((f + d) % 8, s), device_id_type=MESH)
    pl.semaphore_wait(barrier, 13)

    c_sky.wait()
    for d in (2, 1, 3):
        r = piece(a, b)
        push(r, r, k1s.at[d], k1r.at[d], first(d))

    vis = vis_v[...]
    slot_no = iota((8, 36), 1)
    row_no = iota((8, 36), 0)
    lim = jnp.zeros((8, 36), I32)
    for q in range(8):
        lim = jnp.where(row_no == q, cnt[0, q], lim)
    used = slot_no < lim
    src = vis >> 2
    grp = vis & 3
    later = jnp.zeros((8, 36), I32)
    for q in range(16):
        hit = used & (src == q)
        lo = jnp.min(jnp.where(hit, grp, 3))
        hi = jnp.max(jnp.where(hit, grp, 0))
        selb[2 * q:2 * q + 1, :] = jnp.full((1, 128), lo, I32)
        selb[2 * q + 1:2 * q + 2, :] = jnp.full((1, 128), hi, I32)
        later = jnp.where(hit & (grp == hi), 1, later)
    for d in (1, 2, 3):
        push(selb, selp.at[4 - d], ls_s.at[d], ls_r.at[4 - d], second(d))
    sx, sy = src >> 2, src & 3
    ia = sx * (1 - o) + sy * o
    fb = sy * (1 - o) + sx * o
    ent[...] = jnp.zeros((8, 128), I32)
    ent[:, 0:36] = jnp.where(used, fb * 8 + ia * 2 + later, 32)
    c_ent = pltpu.make_async_copy(ent, eidx, lsem.at[0])
    c_ent.start()

    for d in (1, 3, 2):
        arrived(piece(a - d, b), k1s.at[d], k1r.at[d], first(d))
    for c in range(CHUNKS):
        for d in (2, 1, 3):
            r = piece(c - b + 4, b)
            push(r, r, k2s.at[d, c], k2r.at[d, c], second(d))

    c_day.wait()
    for t in range(9):
        dayv[64 * t:64 * t + 64, :] = rawd[16 * t:16 * t + 16].reshape(64, 2305)
    dayv[576:580, :] = rawd[144]

    c_bs.wait()
    for t in range(9):
        bsdfv[64 * t:64 * t + 64, :] = rawb[16 * t:16 * t + 16].reshape(64, 145)
    bsdfv[576:580, :] = rawb[144]
    w1 = (iota((580, 145), 0) // 4 == iota((580, 145), 1)).astype(F32).astype(BF)
    c1 = nt(w1, bsdfv[...]).astype(BF)
    pr, pc = iota((580, 640), 0), iota((580, 640), 1)
    pk, pg = pr // 4, pr % 4
    hit = (pc < 512) & (pc == pg * 128 + pk) & (pk < 128)
    hit = hit | ((pk >= 128) & (pc - 512 == 17 * pg + pk - 128))
    c2 = mm(c1, hit.astype(F32).astype(BF))
    rr = pc - 512
    gcol = jnp.where(pc < 512, pc // 128,
                     (rr >= 17).astype(I32) + (rr >= 34).astype(I32) + (rr >= 51).astype(I32))
    bexp[...] = jnp.where(pg == gcol, c2, 0.0).astype(BF)

    ur, uc = iota((256, 256), 0), iota((256, 256), 1)
    perm[...] = ((uc % 8 == ur // 32) & (uc // 8 == ur % 32)).astype(F32).astype(BF)

    def permute(lo, hi):
        def body(j, carry):
            slot = j % BUFS
            view_copy(j, slot).wait()
            for t in range(5):
                xin = vbuf[slot, 32 * t:32 * t + 32].reshape(256, 256)
                res = mm(perm[...], xin).astype(BF)
                res = res.reshape(8, 32, 256)
                if t < 4:
                    v2m[j // 2, :, pl.ds(pl.multiple_of(128 * (j % 2) + 32 * t, 32), 32), :] = res
                else:
                    v2r[j // 8, :, pl.ds(pl.multiple_of(32 * (j % 8), 32), 32), :] = res

            @pl.when(j + BUFS < 36)
            def _():
                view_copy(j + BUFS, slot).start()
            return carry
        lax.fori_loop(lo, hi, body, 0)

    def gather(c):
        for d in (1, 3, 2):
            arrived(piece(c - b + d + 4, b - d), k2s.at[d, c], k2r.at[d, c], second(d))
        r = skyv.at[o, c]
        push(r, r, kcs.at[c], kcr.at[c], partner)

    def daylit(c):
        arrived(skyv.at[1 - o, c], kcs.at[c], kcr.at[c], partner)
        lhs = jnp.concatenate([skyv[h, c, q] for q in range(4) for h in range(2)], axis=0)
        dt = nt(lhs, dayv[...]).astype(BF)
        e = mm(dt, bexp[...]).astype(BF)
        for q in range(5):
            e1buf[c][a, q] = e[:, 128 * q:128 * q + 128]
        r = e1buf[c].at[a]
        for d in (1, 3):
            push(r, r, p1s.at[c, d], p1r.at[c, d], first(d))

    def across(c, d, at):
        return e1buf[c].at[at % 4, :, pl.ds(0 if d == 1 else HC // 2, HC // 2)]

    def forward(c):
        for d in (1, 3):
            arrived(e1buf[c].at[(a - d) % 4], p1s.at[c, d], p1r.at[c, d], first(d))
            r = across(c, d, a - d + 4)
            push(r, r, p1s.at[c, d - 1], p1r.at[c, d - 1], first(d))

    def make_q(d):
        lane, col = iota((128, 128), 0), iota((128, 128), 1)
        for i in range(4):
            acc = jnp.zeros((128, 128), F32)
            for m in range(2):
                n = 2 * i + m
                if n < 7:
                    sel = selp[d, pl.ds(sid(i, b) * 2 + m, 1), :]
                    hit = (lane - col == 17 * sel - 17 * n) & (col >= 17 * n) & (col < 17 * n + 17)
                    acc = acc + hit.astype(F32)
            qsel[d, 128 * i:128 * i + 128, :] = acc.astype(BF)
        row, lan = iota((32, 128), 0), iota((32, 128), 1)
        sel = selp[d, pl.ds(sid(3, b) * 2 + 1, 1), :]
        qrest[d] = ((lan - row == 17 * sel) & (row < 17)).astype(F32).astype(BF)

    def select(c):
        for d in (1, 3):
            arrived(across(c, d, a + 2), p1s.at[c, d - 1], p1r.at[c, d - 1], first(d))
        lhs = jnp.concatenate([e1buf[c][i, 4] for i in range(4)], axis=1)
        for d in (2, 1, 3, 0):
            for i in range(4):
                planes = [e1buf[c][i, g].astype(F32) for g in range(4)]
                for m in range(2):
                    sel = selp[d, pl.ds(sid(i, b) * 2 + m, 1), :]
                    pick = planes[0]
                    for g in range(1, 4):
                        pick = jnp.where(sel == g, planes[g], pick)
                    pick = pick.astype(BF)
                    if d:
                        s2m[c, d - 1, 2 * i + m] = pick
                    else:
                        r2m[c][b * 8 + 2 * i + m] = pick
            if d:
                push(s2m.at[c, d - 1], r2m[c].at[pl.ds(b * 8, 8)], p2ms.at[c, d], p2mr.at[c, d], second(d))
            rem = mm(lhs, qsel[d]).astype(BF)
            rest = nt(qrest[d], e1buf[c][3, 4]).astype(BF)
            if d:
                s2r[c, d - 1, 0:128] = rem
                s2r[c, d - 1, 128:160] = rest
                push(s2r.at[c, d - 1], r2r.at[c, b], p2rs.at[c, d], p2rr.at[c, d], second(d))
            else:
                r2r[c, b, 0:128] = rem
                r2r[c, b, 128:160] = rest

    def received(c):
        for d in (1, 3, 2):
            j = (b - d) % 4
            arrived(r2m[c].at[pl.ds(j * 8, 8)], p2ms.at[c, d], p2mr.at[c, d], second(d))
            arrived(r2r.at[c, j], p2rs.at[c, d], p2rr.at[c, d], second(d))
        eye = (iota((HC, HC), 0) == iota((HC, HC), 1)).astype(F32).astype(BF)
        wide = (iota((32, 128), 0) == iota((32, 128), 1) % 32).astype(F32).astype(BF)

        def body(fb, carry):
            plane = r2r[c, fb, 0:128]
            for n in range(7):
                trem[fb * 8 + n] = mm(plane, place[n]).astype(BF)
            last = nt(eye, r2r[c, fb, 128:160]).astype(BF)
            trem[fb * 8 + 7] = mm(last, wide).astype(BF)
            return carry
        lax.fori_loop(0, 4, body, 0)

    def dest(i):
        return ((z + 1 + i // 2) % 4) * 2 + (o + 1 + i % 2) % 2

    def compute(c):
        def block(i):
            bb = dest(i)
            acc = None
            es = [eidx[bb, j] for j in range(36)]
            for j in range(18):
                lhs = jnp.concatenate([r2m[c][es[2 * j]], r2m[c][es[2 * j + 1]]], axis=1)
                p = mm(lhs, v2m[j, bb])
                acc = p if acc is None else acc + p
            quarter = iota((HC, 128), 1) // 32
            for q in range(9):
                h = trem[es[4 * q]]
                for k in range(1, 4):
                    h = jnp.where(quarter == k, trem[es[4 * q + k]], h)
                if q % 2 == 0:
                    prev = h
                else:
                    acc = acc + mm(jnp.concatenate([prev, h], axis=1), v2r[q // 2, bb])
            return acc + mm(prev, v2r[4, bb, 0:128])

        def body(i, carry):
            rss[c, i] = block(i).astype(BF)
            pltpu.make_async_remote_copy(
                src_ref=rss.at[c, i], dst_ref=rsr.at[c, i], send_sem=rs_s.at[c], recv_sem=rs_r.at[c],
                device_id=(dest(i), s), device_id_type=MESH).start()
            return carry
        lax.fori_loop(0, 7, body, 0)
        own[c] = block(7)

    def rs_all(c):
        return pltpu.make_async_remote_copy(
            src_ref=rss.at[c], dst_ref=rsr.at[c], send_sem=rs_s.at[c], recv_sem=rs_r.at[c],
            device_id=(dest(0), s), device_id_type=MESH)

    def reduce(c):
        rs_all(c).wait_recv()
        acc = own[c]
        for i in range(7):
            acc = acc + rsr[c, i].astype(F32)
        t = acc.T
        for q in range(4):
            lo = 128 * ((c - q) % 4) + 32 * q
            out[0, :, lo:lo + 32] = t[:, 32 * q:32 * q + 32]

    for c in range(CHUNKS):
        r2m[c][32] = jnp.zeros((HC, 128), BF)
    trem[32] = jnp.zeros((HC, 128), BF)
    for n in range(7):
        place[n] = (iota((128, 128), 0) == iota((128, 128), 1) % 32 + 17 * n).astype(F32).astype(BF) * (
            iota((128, 128), 1) % 32 < 17).astype(F32).astype(BF)
    permute(0, 8)
    gather(0)
    gather(1)
    daylit(0)
    gather(2)
    daylit(1)
    gather(3)
    daylit(2)
    daylit(3)
    selp[0] = selb[...]
    for d in (1, 2, 3):
        arrived(selp.at[d], ls_s.at[d], ls_r.at[d], second(d))
    for d in range(4):
        make_q(d)
    permute(8, 12)
    forward(0)
    forward(1)
    permute(12, 18)
    forward(2)
    select(0)
    forward(3)
    permute(18, 22)
    select(1)
    permute(22, 28)
    select(2)
    permute(28, 36)
    c_ent.wait()
    received(0)
    compute(0)
    select(3)
    for c in range(1, CHUNKS):
        received(c)
        compute(c)
        reduce(c - 1)
    reduce(CHUNKS - 1)
    for cp in sends:
        cp.wait_send()
    for c in range(CHUNKS):
        rs_all(c).wait_send()


def on_device(sky, daylight, bsdf, view, visible, counts):
    V = pltpu.VMEM
    D = pltpu.SemaphoreType.DMA
    anyspec = pl.BlockSpec(memory_space=pl.ANY)
    vm = pl.BlockSpec(memory_space=pltpu.VMEM)
    sm = pl.BlockSpec(memory_space=pltpu.SMEM)
    return pl.pallas_call(
        kernel,
        out_shape=jax.ShapeDtypeStruct((1, 256, 512), F32),
        in_specs=[anyspec, anyspec, anyspec, anyspec, vm, sm],
        out_specs=vm,
        scratch_shapes=[
            V((2, 4, 4, 16, 2305), BF), V((145, 4, 2305), BF), V((145, 4, 145), BF),
            V((580, 2305), BF), V((580, 145), BF), V((580, 640), BF),
            V((BUFS, 160, 8, 256), BF), V((18, 8, 256, 256), BF), V((5, 8, 256, 256), BF),
            *[V((4, 5, HC, 128), BF)] * 4, *[V((33, HC, 128), BF)] * 4,
            V((CHUNKS, 3, 8, HC, 128), BF), V((CHUNKS, 3, 160, 128), BF),
            V((CHUNKS, 4, 160, 128), BF), V((33, HC, 128), BF),
            V((32, 128), I32), V((4, 32, 128), I32), V((4, 512, 128), BF), V((4, 32, 128), BF), V((7, 128, 128), BF),
            V((8, 128), I32), pltpu.SMEM((8, 128), I32),
            V((CHUNKS, 7, HC, 256), BF), V((CHUNKS, 7, HC, 256), BF), V((CHUNKS, HC, 256), F32),
            V((256, 256), BF),
            D((3,)), D((BUFS,)), D((4,)), D((4,)), D((4, 4)), D((4, 4)), D((4,)), D((4,)),
            D((4,)), D((4,)),
            *[D((CHUNKS, 4))] * 6, D((CHUNKS,)), D((CHUNKS,)),
        ],
        compiler_params=pltpu.CompilerParams(
            collective_id=0, has_side_effects=True, vmem_limit_bytes=60 * 2**20),
    )(sky.T, daylight.transpose(1, 0, 2), bsdf.transpose(1, 0, 2), view.transpose(1, 2, 0, 3),
      visible, counts.T)


def solution(mesh):
    placed = (
        P(None, "sensor"),
        P(("facade", "sensor"), None, None),
        P(("facade", "sensor"), None, None),
        P("sensor", "facade", None, None),
        P("sensor", "facade"),
        P("sensor", "facade"),
    )
    return jax.shard_map(
        on_device,
        mesh=mesh,
        in_specs=placed,
        out_specs=P(("sensor", "facade"), None, None),
        check_vma=False,
    )
```

```python
import functools

import jax
import jax.numpy as jnp
from jax import lax
from jax.experimental import pallas as pl
from jax.experimental.pallas import tpu as pltpu
from jax.sharding import PartitionSpec as P

MESH = pl.DeviceIdType.MESH
BF = jnp.bfloat16
F32 = jnp.float32
I32 = jnp.int32

CHUNKS = 4
HC = 128
BUFS = 4


def iota(shape, dim):
    return lax.broadcasted_iota(I32, shape, dim)


def nt(a, b):
    return lax.dot_general(a, b, (((1,), (1,)), ((), ())), preferred_element_type=F32)


def mm(a, b):
    return jnp.dot(a, b, preferred_element_type=F32)


def kernel(sky, day, bsdf, view, vis_v, cnt, out,
           skyv, rawd, rawb, dayv, bsdfv, bexp, vbuf, v2m, v2r,
           e0, e1, e2, e3, m0, m1, m2, m3,
           s2m, s2r, r2r, trem, selb, selp, qsel, qrest, place, ent, eidx, rss, rsr, own, perm,
           lsem, vsem, k1s, k1r, k2s, k2r, kcs, kcr, ls_s, ls_r,
           p1s, p1r, p2ms, p2mr, p2rs, p2rr, rs_s, rs_r):
    e1buf = [e0, e1, e2, e3]
    r2m = [m0, m1, m2, m3]
    f = lax.axis_index("facade")
    s = lax.axis_index("sensor")
    z, o = f // 2, f % 2
    x, y = s // 4, s % 4
    a = x * (1 - o) + y * o
    b = y * (1 - o) + x * o

    def sid(i, j):
        i, j = i % 4, j % 4
        return (i * 4 + j) * (1 - o) + (j * 4 + i) * o

    def first(d):
        return (f, sid(a + d, b))

    def second(d):
        return (f, sid(a, b + d))

    partner = (z * 2 + (1 - o), s)
    sends = []

    def push(src, dst, ss, rs, dev):
        cp = pltpu.make_async_remote_copy(src_ref=src, dst_ref=dst, send_sem=ss, recv_sem=rs,
                                          device_id=dev, device_id_type=MESH)
        cp.start()
        sends.append(cp)

    def arrived(dst, ss, rs, dev):
        pltpu.make_async_remote_copy(src_ref=dst, dst_ref=dst, send_sem=ss, recv_sem=rs,
                                     device_id=dev, device_id_type=MESH).wait_recv()

    def piece(i, j):
        i, j = i % 4, j % 4
        return skyv.at[o, (i + j) % 4, j * (1 - o) + i * o]

    c_sky = pltpu.make_async_copy(sky.at[pl.ds(pl.multiple_of(16 * o, 16), 16)], piece(a, b), lsem.at[0])
    c_sky.start()
    c_bs = pltpu.make_async_copy(bsdf, rawb, lsem.at[2])
    c_bs.start()
    c_day = pltpu.make_async_copy(day, rawd, lsem.at[1])
    c_day.start()

    def view_copy(j, slot):
        return pltpu.make_async_copy(view.at[j], vbuf.at[slot, pl.ds(0, 145)], vsem.at[slot])

    for q in range(BUFS):
        vbuf[q, 145:160] = jnp.zeros((15, 8, 256), BF)
        view_copy(q, q).start()

    barrier = pltpu.get_barrier_semaphore()
    for d in (1, 2, 3):
        pl.semaphore_signal(barrier, inc=1, device_id=first(d), device_id_type=MESH)
        pl.semaphore_signal(barrier, inc=1, device_id=second(d), device_id_type=MESH)
    for d in range(1, 8):
        pl.semaphore_signal(barrier, inc=1, device_id=((f + d) % 8, s), device_id_type=MESH)
    pl.semaphore_wait(barrier, 13)

    c_sky.wait()
    for d in (2, 1, 3):
        r = piece(a, b)
        push(r, r, k1s.at[d], k1r.at[d], first(d))

    vis = vis_v[...]
    slot_no = iota((8, 36), 1)
    row_no = iota((8, 36), 0)
    lim = jnp.zeros((8, 36), I32)
    for q in range(8):
        lim = jnp.where(row_no == q, cnt[0, q], lim)
    used = slot_no < lim
    src = vis >> 2
    grp = vis & 3
    later = jnp.zeros((8, 36), I32)
    for q in range(16):
        hit = used & (src == q)
        lo = jnp.min(jnp.where(hit, grp, 3))
        hi = jnp.max(jnp.where(hit, grp, 0))
        selb[2 * q:2 * q + 1, :] = jnp.full((1, 128), lo, I32)
        selb[2 * q + 1:2 * q + 2, :] = jnp.full((1, 128), hi, I32)
        later = jnp.where(hit & (grp == hi), 1, later)
    for d in (1, 2, 3):
        push(selb, selp.at[4 - d], ls_s.at[d], ls_r.at[4 - d], second(d))
    sx, sy = src >> 2, src & 3
    ia = sx * (1 - o) + sy * o
    fb = sy * (1 - o) + sx * o
    ent[...] = jnp.zeros((8, 128), I32)
    ent[:, 0:36] = jnp.where(used, fb * 8 + ia * 2 + later, 32)
    c_ent = pltpu.make_async_copy(ent, eidx, lsem.at[0])
    c_ent.start()

    for d in (1, 3, 2):
        arrived(piece(a - d, b), k1s.at[d], k1r.at[d], first(d))
    for c in range(CHUNKS):
        for d in (2, 1, 3):
            r = piece(c - b + 4, b)
            push(r, r, k2s.at[d, c], k2r.at[d, c], second(d))

    c_day.wait()
    for t in range(9):
        dayv[64 * t:64 * t + 64, :] = rawd[16 * t:16 * t + 16].reshape(64, 2305)
    dayv[576:580, :] = rawd[144]

    c_bs.wait()
    for t in range(9):
        bsdfv[64 * t:64 * t + 64, :] = rawb[16 * t:16 * t + 16].reshape(64, 145)
    bsdfv[576:580, :] = rawb[144]
    w1 = (iota((580, 145), 0) // 4 == iota((580, 145), 1)).astype(F32).astype(BF)
    c1 = nt(w1, bsdfv[...]).astype(BF)
    pr, pc = iota((580, 640), 0), iota((580, 640), 1)
    pk, pg = pr // 4, pr % 4
    hit = (pc < 512) & (pc == pg * 128 + pk) & (pk < 128)
    hit = hit | ((pk >= 128) & (pc - 512 == 17 * pg + pk - 128))
    c2 = mm(c1, hit.astype(F32).astype(BF))
    rr = pc - 512
    gcol = jnp.where(pc < 512, pc // 128,
                     (rr >= 17).astype(I32) + (rr >= 34).astype(I32) + (rr >= 51).astype(I32))
    bexp[...] = jnp.where(pg == gcol, c2, 0.0).astype(BF)

    ur, uc = iota((256, 256), 0), iota((256, 256), 1)
    perm[...] = ((uc % 8 == ur // 32) & (uc // 8 == ur % 32)).astype(F32).astype(BF)

    def permute(lo, hi):
        def body(j, carry):
            slot = j % BUFS
            view_copy(j, slot).wait()
            for t in range(5):
                xin = vbuf[slot, 32 * t:32 * t + 32].reshape(256, 256)
                res = mm(perm[...], xin).astype(BF)
                res = res.reshape(8, 32, 256)
                if t < 4:
                    v2m[j // 2, :, pl.ds(pl.multiple_of(128 * (j % 2) + 32 * t, 32), 32), :] = res
                else:
                    v2r[j // 8, :, pl.ds(pl.multiple_of(32 * (j % 8), 32), 32), :] = res

            @pl.when(j + BUFS < 36)
            def _():
                view_copy(j + BUFS, slot).start()
            return carry
        lax.fori_loop(lo, hi, body, 0)

    def gather(c):
        for d in (1, 3, 2):
            arrived(piece(c - b + d + 4, b - d), k2s.at[d, c], k2r.at[d, c], second(d))
        r = skyv.at[o, c]
        push(r, r, kcs.at[c], kcr.at[c], partner)

    def daylit(c):
        arrived(skyv.at[1 - o, c], kcs.at[c], kcr.at[c], partner)
        lhs = jnp.concatenate([skyv[h, c, q] for q in range(4) for h in range(2)], axis=0)
        dt = nt(lhs, dayv[...]).astype(BF)
        e = mm(dt, bexp[...]).astype(BF)
        for q in range(5):
            e1buf[c][a, q] = e[:, 128 * q:128 * q + 128]
        r = e1buf[c].at[a]
        for d in (1, 3):
            push(r, r, p1s.at[c, d], p1r.at[c, d], first(d))

    def across(c, d, at):
        return e1buf[c].at[at % 4, :, pl.ds(0 if d == 1 else HC // 2, HC // 2)]

    def forward(c):
        for d in (1, 3):
            arrived(e1buf[c].at[(a - d) % 4], p1s.at[c, d], p1r.at[c, d], first(d))
            r = across(c, d, a - d + 4)
            push(r, r, p1s.at[c, d - 1], p1r.at[c, d - 1], first(d))

    def make_q(d):
        lane, col = iota((128, 128), 0), iota((128, 128), 1)
        for i in range(4):
            acc = jnp.zeros((128, 128), F32)
            for m in range(2):
                n = 2 * i + m
                if n < 7:
                    sel = selp[d, pl.ds(sid(i, b) * 2 + m, 1), :]
                    hit = (lane - col == 17 * sel - 17 * n) & (col >= 17 * n) & (col < 17 * n + 17)
                    acc = acc + hit.astype(F32)
            qsel[d, 128 * i:128 * i + 128, :] = acc.astype(BF)
        row, lan = iota((32, 128), 0), iota((32, 128), 1)
        sel = selp[d, pl.ds(sid(3, b) * 2 + 1, 1), :]
        qrest[d] = ((lan - row == 17 * sel) & (row < 17)).astype(F32).astype(BF)

    def select(c):
        for d in (1, 3):
            arrived(across(c, d, a + 2), p1s.at[c, d - 1], p1r.at[c, d - 1], first(d))
        lhs = jnp.concatenate([e1buf[c][i, 4] for i in range(4)], axis=1)
        for d in (2, 1, 3, 0):
            for i in range(4):
                planes = [e1buf[c][i, g].astype(F32) for g in range(4)]
                for m in range(2):
                    sel = selp[d, pl.ds(sid(i, b) * 2 + m, 1), :]
                    pick = planes[0]
                    for g in range(1, 4):
                        pick = jnp.where(sel == g, planes[g], pick)
                    pick = pick.astype(BF)
                    if d:
                        s2m[c, d - 1, 2 * i + m] = pick
                    else:
                        r2m[c][b * 8 + 2 * i + m] = pick
            if d:
                push(s2m.at[c, d - 1], r2m[c].at[pl.ds(b * 8, 8)], p2ms.at[c, d], p2mr.at[c, d], second(d))
            rem = mm(lhs, qsel[d]).astype(BF)
            rest = nt(qrest[d], e1buf[c][3, 4]).astype(BF)
            if d:
                s2r[c, d - 1, 0:128] = rem
                s2r[c, d - 1, 128:160] = rest
                push(s2r.at[c, d - 1], r2r.at[c, b], p2rs.at[c, d], p2rr.at[c, d], second(d))
            else:
                r2r[c, b, 0:128] = rem
                r2r[c, b, 128:160] = rest

    def received(c):
        for d in (1, 3, 2):
            j = (b - d) % 4
            arrived(r2m[c].at[pl.ds(j * 8, 8)], p2ms.at[c, d], p2mr.at[c, d], second(d))
            arrived(r2r.at[c, j], p2rs.at[c, d], p2rr.at[c, d], second(d))
        eye = (iota((HC, HC), 0) == iota((HC, HC), 1)).astype(F32).astype(BF)
        wide = (iota((32, 128), 0) == iota((32, 128), 1) % 32).astype(F32).astype(BF)

        def body(fb, carry):
            plane = r2r[c, fb, 0:128]
            for n in range(7):
                trem[fb * 8 + n] = mm(plane, place[n]).astype(BF)
            last = nt(eye, r2r[c, fb, 128:160]).astype(BF)
            trem[fb * 8 + 7] = mm(last, wide).astype(BF)
            return carry
        for fb in range(4):
            body(fb, 0)

    def dest(i):
        return ((z + 1 + i // 2) % 4) * 2 + (o + 1 + i % 2) % 2

    def compute(c):
        def block(i):
            bb = dest(i)
            acc = None
            es = [eidx[bb, j] for j in range(36)]
            for j in range(18):
                lhs = jnp.concatenate([r2m[c][es[2 * j]], r2m[c][es[2 * j + 1]]], axis=1)
                p = mm(lhs, v2m[j, bb])
                acc = p if acc is None else acc + p
            quarter = iota((HC, 128), 1) // 32
            for q in range(9):
                h = trem[es[4 * q]]
                for k in range(1, 4):
                    h = jnp.where(quarter == k, trem[es[4 * q + k]], h)
                if q % 2 == 0:
                    prev = h
                else:
                    acc = acc + mm(jnp.concatenate([prev, h], axis=1), v2r[q // 2, bb])
            return acc + mm(prev, v2r[4, bb, 0:128])

        def body(k, carry):
            i = 2 * k
            even, odd = block(i), block(i + 1)
            rss[c, i] = even.astype(BF)
            rs_copy(c, i).start()
            own[c] = odd

            @pl.when(k < 3)
            def _():
                rss[c, i + 1] = odd.astype(BF)
                rs_copy(c, i + 1).start()
            return carry
        lax.fori_loop(0, 4, body, 0)

    def rs_copy(c, i):
        return pltpu.make_async_remote_copy(
            src_ref=rss.at[c, i], dst_ref=rsr.at[c, i], send_sem=rs_s.at[c], recv_sem=rs_r.at[c],
            device_id=(dest(i), s), device_id_type=MESH)

    def rs_all(c):
        return pltpu.make_async_remote_copy(
            src_ref=rss.at[c], dst_ref=rsr.at[c], send_sem=rs_s.at[c], recv_sem=rs_r.at[c],
            device_id=(dest(0), s), device_id_type=MESH)

    def reduce(c):
        rs_all(c).wait_recv()
        acc = own[c]
        for i in range(7):
            acc = acc + rsr[c, i].astype(F32)
        t = acc.T
        for q in range(4):
            lo = 128 * ((c - q) % 4) + 32 * q
            out[0, :, lo:lo + 32] = t[:, 32 * q:32 * q + 32]

    for c in range(CHUNKS):
        r2m[c][32] = jnp.zeros((HC, 128), BF)
    trem[32] = jnp.zeros((HC, 128), BF)
    for n in range(7):
        place[n] = (iota((128, 128), 0) == iota((128, 128), 1) % 32 + 17 * n).astype(F32).astype(BF) * (
            iota((128, 128), 1) % 32 < 17).astype(F32).astype(BF)
    permute(0, 8)
    gather(0)
    gather(1)
    daylit(0)
    gather(2)
    daylit(1)
    gather(3)
    daylit(2)
    daylit(3)
    selp[0] = selb[...]
    for d in (1, 2, 3):
        arrived(selp.at[d], ls_s.at[d], ls_r.at[d], second(d))
    for d in range(4):
        make_q(d)
    permute(8, 12)
    forward(0)
    forward(1)
    permute(12, 18)
    forward(2)
    select(0)
    forward(3)
    permute(18, 22)
    select(1)
    permute(22, 28)
    select(2)
    permute(28, 36)
    c_ent.wait()
    received(0)
    compute(0)
    select(3)
    for c in range(1, CHUNKS):
        received(c)
        compute(c)
        reduce(c - 1)
    reduce(CHUNKS - 1)
    for cp in sends:
        cp.wait_send()
    for c in range(CHUNKS):
        rs_all(c).wait_send()


def on_device(sky, daylight, bsdf, view, visible, counts):
    V = pltpu.VMEM
    D = pltpu.SemaphoreType.DMA
    anyspec = pl.BlockSpec(memory_space=pl.ANY)
    vm = pl.BlockSpec(memory_space=pltpu.VMEM)
    sm = pl.BlockSpec(memory_space=pltpu.SMEM)
    return pl.pallas_call(
        kernel,
        out_shape=jax.ShapeDtypeStruct((1, 256, 512), F32),
        in_specs=[anyspec, anyspec, anyspec, anyspec, vm, sm],
        out_specs=vm,
        scratch_shapes=[
            V((2, 4, 4, 16, 2305), BF), V((145, 4, 2305), BF), V((145, 4, 145), BF),
            V((580, 2305), BF), V((580, 145), BF), V((580, 640), BF),
            V((BUFS, 160, 8, 256), BF), V((18, 8, 256, 256), BF), V((5, 8, 256, 256), BF),
            *[V((4, 5, HC, 128), BF)] * 4, *[V((33, HC, 128), BF)] * 4,
            V((CHUNKS, 3, 8, HC, 128), BF), V((CHUNKS, 3, 160, 128), BF),
            V((CHUNKS, 4, 160, 128), BF), V((33, HC, 128), BF),
            V((32, 128), I32), V((4, 32, 128), I32), V((4, 512, 128), BF), V((4, 32, 128), BF), V((7, 128, 128), BF),
            V((8, 128), I32), pltpu.SMEM((8, 128), I32),
            V((CHUNKS, 7, HC, 256), BF), V((CHUNKS, 7, HC, 256), BF), V((CHUNKS, HC, 256), F32),
            V((256, 256), BF),
            D((3,)), D((BUFS,)), D((4,)), D((4,)), D((4, 4)), D((4, 4)), D((4,)), D((4,)),
            D((4,)), D((4,)),
            *[D((CHUNKS, 4))] * 6, D((CHUNKS,)), D((CHUNKS,)),
        ],
        compiler_params=pltpu.CompilerParams(
            collective_id=0, has_side_effects=True, vmem_limit_bytes=60 * 2**20),
    )(sky.T, daylight.transpose(1, 0, 2), bsdf.transpose(1, 0, 2), view.transpose(1, 2, 0, 3),
      visible, counts.T)


def solution(mesh):
    placed = (
        P(None, "sensor"),
        P(("facade", "sensor"), None, None),
        P(("facade", "sensor"), None, None),
        P("sensor", "facade", None, None),
        P("sensor", "facade"),
        P("sensor", "facade"),
    )
    return jax.shard_map(
        on_device,
        mesh=mesh,
        in_specs=placed,
        out_specs=P(("sensor", "facade"), None, None),
        check_vma=False,
    )
```
